32 devices in a mesh: head: 4 (over z), page: 8 (over y, x, core).
Axes of the slice: x: 2, y: 2, z: 4, core: 2. Of those that a mesh axis runs over, the one named last changes fastest.
Arguments:
- hidden_in: bfloat16 [8, 1024, 1024], P('page', 'head'), may hold values from -6 to 6
- norm_gain: float32 [1024], replicated, may hold values from 0.1 to 1.9
- w_qkv: bfloat16 [1024, 3, 1024], P(None, None, 'head'), may hold values from -0.1875 to 0.1875
- w_out: bfloat16 [1024, 1024], P('head'), may hold values from -0.75 to 0.75
- cache_kv: bfloat16 [2, 16, 128, 1024], P(None, 'page', None, 'head'), may hold values from -110 to 110, as said below
- page_node: int32 [16], replicated, may hold values from 0 to 6, as said below
- page_fill: int32 [16], replicated, may hold values from 1 to 128
- node_parent: int32 [7], replicated, may hold values from 0 to 2, as said below
- tok_seg: int32 [8, 1024], P('page'), may hold values from 0 to 7, never falling along the last dimension, each value on 1 to 256 neighbouring positions
- req_leaf: int32 [8, 8], P('page'), may hold values from 3 to 6, as said below
Outputs:
- attn_out: bfloat16 [8, 1024, 1024], P('page', 'head')
The draws below stay inside these ranges and needn't reach their ends.
Inputs may be any that keep to these rules, and one draw needn't show every extreme that they name: `cache_kv`: entries of the cache; keys and values. `page_node`: every node owns at least one page. `node_parent`: node 0 is the root and its own parent; nodes 1 to 2 have parent 0; the others have a parent among nodes 1 to 2, and each of those has a child. `req_leaf`: each request names a lowest-level node; every lowest-level node is named by some request.
All inputs are finite; a program needn't handle non-finite values.
Results may differ from the reference program's by a relative error of at most 0.018.
Values may be sent and summed in bfloat16 or wider, within the bound.
A program may use at most 64 MiB of HBM per device.

```python
import math
import jax
import jax.numpy as jnp
import numpy as np
from jax import lax

D = 1024
H = 16
HD = 64
PAGE = 128
SEGS = 8
BRANCHES = 2
TQ = 1024
MOST = 256
SHARDS = 8
PAGES = 16
LEAVES = 4
NODES = 7
N_PAGE = 8


def draw_cache_kv(key, part):
    key_base = jax.random.fold_in(key, 0)
    shape = (2, PAGES, PAGE, H, HD)
    whole = jnp.clip(jax.random.normal(key_base, shape, jnp.float32), -4.0, 4.0)
    return whole.reshape(2, PAGES, PAGE, H * HD).astype(jnp.bfloat16)


def draw_page_node(key, part):
    key_rest, key_order = jax.random.split(jax.random.fold_in(key, 11), 2)
    covered = jnp.arange(NODES, dtype=jnp.int32)
    others = jax.random.randint(key_rest, (PAGES - NODES,), 0, NODES, dtype=jnp.int32)
    return jax.random.permutation(key_order, jnp.concatenate([covered, others])).astype(jnp.int32)


def draw_page_fill(key, part):
    key_pick, key_fill = jax.random.split(jax.random.fold_in(key, 12), 2)
    partial_page = jax.random.randint(key_pick, (PAGES,), 0, 2, dtype=jnp.int32) == 0
    fill_values = jax.random.randint(key_fill, (PAGES,), 1, PAGE + 1, dtype=jnp.int32)
    fill_values = jnp.where(partial_page, fill_values, PAGE)
    return jnp.where(jnp.arange(PAGES, dtype=jnp.int32) == 0, PAGE, fill_values).astype(jnp.int32)


def draw_node_parent(key, part):
    order = jax.random.permutation(jax.random.fold_in(key, 13), LEAVES).astype(jnp.int32)
    lower = 1 + order % BRANCHES
    upper = jnp.zeros((1 + BRANCHES,), jnp.int32)
    return jnp.concatenate([upper, lower]).astype(jnp.int32)


def draw_req_leaf(key, part):
    order = jax.random.permutation(jax.random.fold_in(key, 14), N_PAGE * SEGS).astype(jnp.int32)
    return (1 + BRANCHES + order % LEAVES).reshape(N_PAGE, SEGS).astype(jnp.int32)


def shard_levels(stream_key, shape, shards, low, top_value):
    loudness = 1.0
    for axis_at, blocks in shards:
        steps = jax.random.uniform(jax.random.fold_in(jax.random.fold_in(stream_key, 6), axis_at), (blocks,), jnp.float32, low / len(shards), top_value / len(shards))
        loudness = loudness * jnp.repeat(jnp.exp(steps), shape[axis_at] // blocks).reshape((-1,) + (1,) * (len(shape) - 1 - axis_at))
    return loudness


def profile(count, total, limit, slope):
    weights = [(1 << 20) // math.isqrt(grade ** slope) + 1 for grade in range(2, count + 1)]
    spare, counts = total - limit - (count - 1), [1] * (count - 1)
    while spare > 0:
        movable = [i for i in range(count - 1) if counts[i] < limit]
        whole, remaining = sum([weights[i] for i in movable]), spare
        for i in movable:
            more = min(limit - counts[i], max(1, remaining * weights[i] // whole), spare)
            counts[i] = counts[i] + more
            spare = spare - more
    return np.array([limit] + counts)


def uneven_parts(own_key, number_of, total, reach, skew):
    if number_of == 2:
        one = jax.random.randint(own_key, (), max(1, total - reach), min(reach, total - 1) + 1)
        return jnp.stack([one, total - one])
    sizes = jnp.asarray(profile(number_of, total, reach, skew), jnp.int32)
    pairs = (number_of - 1) // 2
    donor, receiver = sizes[1:1 + 2 * pairs:2], sizes[2:2 + 2 * pairs:2]
    margin = jnp.minimum(donor - 1, reach - receiver)
    passed = jax.random.randint(jax.random.fold_in(own_key, 1), (pairs,), 0, 1 << 20) % (margin + 1)
    sizes = sizes.at[1:1 + 2 * pairs:2].set(donor - passed).at[2:2 + 2 * pairs:2].set(receiver + passed)
    return sizes[jax.random.permutation(jax.random.fold_in(own_key, 2), number_of)]


def bell_draw(stream_key, dims, deviation, limit, shards=(), held_as=jnp.bfloat16):
    array = deviation * jax.random.normal(stream_key, dims, jnp.float32)
    if shards:
        array = array * shard_levels(stream_key, dims, shards, -0.22, 0.18)
    return jnp.clip(array, -limit, limit).astype(held_as)


def setup_inputs(seed: int = 0) -> dict:
    key_of = jax.random.split(jax.random.key(seed), 11)
    hidden_in = bell_draw(key_of[0], (SHARDS, TQ, D), 1.0, 6.0, ((0, 8), (1, 4)))
    norm_gain = jnp.clip(1.0 + 0.18 * jax.random.normal(key_of[1], (D,), jnp.float32), 0.1, 1.9)
    w_qkv = bell_draw(key_of[2], (D, 3, H * HD), D ** -0.5, 0.1875, ((2, 4),))
    w_out = bell_draw(key_of[3], (H * HD, D), HD ** -0.5, 0.75, ((0, 4),))
    cache_kv = draw_cache_kv(jax.random.fold_in(key_of[10], 71), 0)
    page_node = draw_page_node(jax.random.fold_in(key_of[10], 71), 0)
    page_fill = draw_page_fill(jax.random.fold_in(key_of[10], 71), 0)
    node_parent = draw_node_parent(jax.random.fold_in(key_of[10], 71), 0)
    tok_seg = jax.vmap(lambda own: jnp.searchsorted(jnp.cumsum(uneven_parts(own, SEGS, TQ, MOST, 2)), jnp.arange(TQ), side="right"))(jax.random.split(key_of[8], SHARDS)).reshape((SHARDS, TQ)).astype(jnp.int32)
    req_leaf = draw_req_leaf(jax.random.fold_in(key_of[10], 71), 0)
    return dict(hidden_in=hidden_in, norm_gain=norm_gain, w_qkv=w_qkv, w_out=w_out, cache_kv=cache_kv, page_node=page_node, page_fill=page_fill, node_parent=node_parent, tok_seg=tok_seg, req_leaf=req_leaf)


EPSILON = 1e-06
FLOOR_SCORE = -1e+30

def reference(hidden_in, norm_gain, w_qkv, w_out, cache_kv, page_node, page_fill, node_parent, tok_seg, req_leaf):
    key_count = PAGES * PAGE
    cache_keys = jnp.transpose(cache_kv[0].reshape(key_count, H, HD), (1, 0, 2))
    cache_values = jnp.transpose(cache_kv[1].reshape(key_count, H, HD), (1, 0, 2))
    key_node = jnp.repeat(page_node, PAGE).astype(jnp.int32)
    slot_ok = (jnp.arange(PAGE, dtype=jnp.int32)[None, :] < page_fill[:, None]).reshape(key_count)
    position = jnp.arange(TQ, dtype=jnp.int32)

    def shard_out(inputs):
        shard_rows, segment, leaves = inputs
        widened = shard_rows.astype(jnp.float32)
        normed = (widened * lax.rsqrt(lax.optimization_barrier(jnp.mean(widened * widened, axis=1, keepdims=True)) + EPSILON) * norm_gain).astype(jnp.bfloat16)
        projected = jnp.dot(normed, w_qkv.reshape(D, 3 * H * HD), preferred_element_type=jnp.float32).astype(jnp.bfloat16)
        projected = jnp.transpose(projected.reshape(TQ, 3, H, HD), (1, 2, 0, 3))
        leaf_node = leaves[segment].astype(jnp.int32)
        upper_node = node_parent[leaf_node].astype(jnp.int32)
        root_node = node_parent[upper_node].astype(jnp.int32)
        prefix_seen = ((key_node[None, :] == leaf_node[:, None]) | (key_node[None, :] == upper_node[:, None]) | (key_node[None, :] == root_node[:, None])) & slot_ok[None, :]
        suffix_seen = (segment[:, None] == segment[None, :]) & (position[None, :] <= position[:, None])
        visible = jnp.concatenate([prefix_seen, suffix_seen], axis=1)

        def head_out(head_inputs):
            queries, new_keys, new_values, old_keys, old_values = head_inputs
            all_keys = jnp.concatenate([old_keys, new_keys], axis=0)
            all_values = jnp.concatenate([old_values, new_values], axis=0)
            scores = jnp.dot(queries, all_keys.T, preferred_element_type=jnp.float32) * HD ** (-0.5)
            scores = jnp.where(visible, scores, FLOOR_SCORE)
            row_max = lax.optimization_barrier(jnp.max(scores, axis=1, keepdims=True))
            expo = jnp.where(visible, jnp.exp(scores - row_max), 0.0)
            row_sum = lax.optimization_barrier(jnp.sum(expo, axis=1, keepdims=True))
            weighted = jnp.dot(expo.astype(jnp.bfloat16), all_values, preferred_element_type=jnp.float32)
            return (weighted / row_sum).astype(jnp.bfloat16)
        head_outputs = lax.map(head_out, (projected[0], projected[1], projected[2], cache_keys, cache_values))
        attention = jnp.transpose(head_outputs, (1, 0, 2)).reshape(TQ, H * HD)
        return jnp.dot(attention, w_out, preferred_element_type=jnp.float32).astype(jnp.bfloat16)
    return lax.map(shard_out, (hidden_in, tok_seg, req_leaf))
```

```python
import functools

import jax
import jax.numpy as jnp
from jax import lax
from jax.experimental import pallas as pl
from jax.experimental.pallas import tpu as pltpu
from jax.sharding import PartitionSpec as P

HD = 64
EPSILON = 1e-06
BIG = 1e30
KEY_BLOCK = 2048
SPLIT = 8
MESH = pl.DeviceIdType.MESH
F32 = jnp.float32
BF16 = jnp.bfloat16


def dot_t(a, b):
    return lax.dot_general(a, b, (((1,), (1,)), ((), ())), preferred_element_type=F32)


def dot(a, b):
    return jnp.dot(a, b, preferred_element_type=F32)


def kernel(
    dims,
    hid,
    gain,
    w,
    wo,
    cache,
    page_node,
    page_fill,
    parent,
    seg,
    leaf,
    out,
    normed,
    cache_all,
    wo_rel,
    qa,
    ka,
    va,
    kp,
    vp,
    acc,
    top,
    qext,
    kext,
    attn,
    attn_rel,
    x_send,
    x_recv,
    c_send,
    c_fwd,
    c_recv,
    wz_send,
    wz_recv,
    wp_send,
    wp_recv,
    a_send,
    a_recv,
):
    n_head, n_page, n_nodes, n_segs = dims
    h = lax.axis_index("head")
    p = lax.axis_index("page")
    rows = hid.shape[0]
    width = w.shape[1] // 3
    heads = width // HD
    dev_pages, page_len = cache.shape[1], cache.shape[2]
    half = n_page // 2
    sibling = p + 1 - 2 * lax.rem(p, 2)
    slice_rows = wo.shape[0] // SPLIT
    my_slice = lax.rem(p, SPLIT)
    group = p - my_slice

    barrier = pltpu.get_barrier_semaphore()
    for d in range(1, n_head):
        pl.semaphore_signal(
            barrier, inc=1, device_id=(lax.rem(h + d, n_head), p), device_id_type=MESH
        )

    @pl.loop(1, n_page)
    def _(k):
        pl.semaphore_signal(
            barrier, inc=1, device_id=(h, lax.rem(p + k, n_page)), device_id_type=MESH
        )

    wide = hid[...].astype(F32)
    scale = lax.rsqrt(jnp.mean(wide * wide, axis=1, keepdims=True) + EPSILON)
    normed[h] = (wide * scale * gain[...]).astype(BF16)
    pl.semaphore_wait(barrier, n_head - 1 + n_page - 1)

    def x_copy(c, way, target):
        return pltpu.make_async_remote_copy(
            src_ref=normed.at[c],
            dst_ref=normed.at[c],
            send_sem=x_send.at[way, c],
            recv_sem=x_recv.at[c],
            device_id=(target, p),
            device_id_type=MESH,
        )

    def c_copy(src, slot, sem, target):
        return pltpu.make_async_remote_copy(
            src_ref=src,
            dst_ref=cache_all.at[slot],
            send_sem=sem,
            recv_sem=c_recv.at[slot],
            device_id=(h, target),
            device_id_type=MESH,
        )

    def wz_copy(d):
        part = pl.ds(pl.multiple_of(my_slice * slice_rows, slice_rows), slice_rows)
        return pltpu.make_async_remote_copy(
            src_ref=wo.at[part],
            dst_ref=wo_rel.at[d - 1, part],
            send_sem=wz_send.at[d - 1],
            recv_sem=wz_recv.at[d - 1],
            device_id=(lax.rem(h + n_head - d, n_head), p),
            device_id_type=MESH,
        )

    def wp_copy(owner, target):
        part = pl.ds(pl.multiple_of(owner * slice_rows, slice_rows), slice_rows)
        block = wo_rel.at[:, part]
        return pltpu.make_async_remote_copy(
            src_ref=block,
            dst_ref=block,
            send_sem=wp_send.at[target],
            recv_sem=wp_recv.at[owner],
            device_id=(h, group + target),
            device_id_type=MESH,
        )

    def a_copy(c, d):
        return pltpu.make_async_remote_copy(
            src_ref=attn.at[c],
            dst_ref=attn_rel.at[d - 1],
            send_sem=a_send.at[c],
            recv_sem=a_recv.at[d - 1],
            device_id=(c, p),
            device_id_type=MESH,
        )

    @pl.when(h > 0)
    def _():
        x_copy(h, 0, h - 1).start()

    @pl.when(h < n_head - 1)
    def _():
        x_copy(h, 1, h + 1).start()

    @pl.loop(1, half)
    def _(k):
        c_copy(cache, p, c_send.at[k], lax.rem(p + 2 * k, n_page)).start()

    c_copy(cache, p, c_fwd.at[0], sibling).start()
    for d in range(1, n_head):
        wz_copy(d).start()

    lane8 = lax.broadcasted_iota(jnp.int32, (n_segs, 128), 1) & (HD - 1)
    row8 = lax.broadcasted_iota(jnp.int32, (n_segs, 128), 0)
    on_path = lane8 < 0
    for s in range(n_segs):
        low = leaf[0, s]
        mid = parent[low]
        root = parent[mid]
        hit = (lane8 == low) | (lane8 == mid) | (lane8 == root)
        on_path = on_path | (hit & (row8 == s))
    own_lane = lane8 == row8 + (n_nodes + 1)
    used = lane8 < n_nodes + 1 + n_segs
    table_q = jnp.where(used & ~on_path & ~own_lane, 1.0, 0.0)
    table_k = jnp.where(own_lane, -BIG, 0.0)
    tokens = seg.shape[1]
    member = seg[...] == lax.broadcasted_iota(jnp.int32, (n_segs, tokens), 0)
    member = jnp.where(member, 1.0, 0.0)
    turned = (((0,), (0,)), ((), ()))
    ext = lax.dot_general(member, table_q, turned, preferred_element_type=F32)
    qext[...] = ext.reshape(qext.shape)
    ext = lax.dot_general(member, table_k, turned, preferred_element_type=F32)
    kext[...] = ext.reshape(kext.shape)

    def project(c):
        x = normed[c]
        low = lax.broadcasted_iota(jnp.int32, (rows, 128), 1) < HD
        q = dot(x, w[:, :width]).astype(BF16).astype(F32) * HD ** (-0.5)
        k = dot(x, w[:, width : 2 * width])
        v = dot(x, w[:, 2 * width :])
        q_more, k_more = qext[c], kext[c]
        for i in range(heads // 2):
            part = slice(i * 128, (i + 1) * 128)
            qa[2 * i, c] = jnp.where(low, q[:, part], q_more).astype(BF16)
            qa[2 * i + 1, c] = jnp.where(low, q_more, q[:, part]).astype(BF16)
            ka[2 * i, c] = jnp.where(low, k[:, part], k_more).astype(BF16)
            ka[2 * i + 1, c] = jnp.where(low, k_more, k[:, part]).astype(BF16)
            va[2 * i, c] = jnp.where(low, v[:, part], 1.0).astype(BF16)
            va[2 * i + 1, c] = jnp.where(low, 1.0, v[:, part]).astype(BF16)

    def widen_page(g, source, i):
        lane = lax.broadcasted_iota(jnp.int32, (page_len, 128), 1)
        low, slot = lane < HD, lax.broadcasted_iota(jnp.int32, (page_len, 128), 0)
        lane = lane & (HD - 1)
        hidden = (lane == page_node[g]) | ((lane == n_nodes) & (slot >= page_fill[g]))
        more = jnp.where(hidden, -BIG, 0.0)
        for j in range(heads // 2):
            part = slice(j * 128, (j + 1) * 128)
            k = cache_all[source, 0, i, :, part].astype(F32)
            v = cache_all[source, 1, i, :, part].astype(F32)
            kp[2 * j, g] = jnp.where(low, k, more).astype(BF16)
            kp[2 * j + 1, g] = jnp.where(low, more, k).astype(BF16)
            vp[2 * j, g] = jnp.where(low, v, 1.0).astype(BF16)
            vp[2 * j + 1, g] = jnp.where(low, 1.0, v).astype(BF16)

    def take_cache():
        @pl.loop(1, half)
        def _(k):
            source = lax.rem(p + 2 * k, n_page)
            c_copy(cache, source, c_send.at[k], sibling).wait_recv()
            c_copy(cache_all.at[source], source, c_fwd.at[k], sibling).start()

        @pl.loop(0, half)
        def _(k):
            source = lax.rem(sibling + 2 * k, n_page)
            c_copy(cache, source, c_fwd.at[0], sibling).wait_recv()

        cache_all[p] = cache[...]

        @pl.loop(0, n_page)
        def _(source):
            for i in range(dev_pages):
                widen_page(source * dev_pages + i, source, i)

    n_keys = n_page * dev_pages * page_len
    block = min(KEY_BLOCK, n_keys)
    block_pages = block // page_len
    blocks = n_keys // block

    def prefix(c):
        @pl.loop(0, heads)
        def _(i):
            q = qa[i, c]

            def scores(b):
                at = pl.ds(b * block_pages, block_pages)
                s = dot_t(q, kp[i, at].reshape(block, 128))
                return s, vp[i, at].reshape(block, 128)

            s, v = scores(0)
            m = jnp.max(s, axis=1, keepdims=True)
            acc[i, c] = dot(jnp.exp(s - m).astype(BF16), v)
            top[i, c] = jnp.broadcast_to(m, (rows, 128))
            if blocks > 1:

                @pl.loop(1, blocks)
                def _(b):
                    s, v = scores(b)
                    old = top[i, c][:, :1]
                    m = jnp.maximum(old, jnp.max(s, axis=1, keepdims=True))
                    acc[i, c] = acc[i, c] * jnp.exp(old - m) + dot(
                        jnp.exp(s - m).astype(BF16), v
                    )
                    top[i, c] = jnp.broadcast_to(m, (rows, 128))

    def finish(c):
        before = jnp.maximum(c - 1, 0)
        shut = jnp.where(c > 0, 0.0, -BIG)
        low = lax.broadcasted_iota(jnp.int32, (rows, 128), 1) < HD
        at = lax.broadcasted_iota(jnp.int32, (rows, rows), 0)
        seen = lax.broadcasted_iota(jnp.int32, (rows, rows), 1) <= at

        def one(i):
            q = qa[i, c]
            near = jnp.where(seen, dot_t(q, ka[i, c]), -BIG)
            far = dot_t(q, ka[i, before]) + shut
            old = top[i, c][:, :1]
            m = jnp.maximum(old, jnp.max(jnp.maximum(near, far), axis=1, keepdims=True))
            total = (
                acc[i, c] * jnp.exp(old - m)
                + dot(jnp.exp(near - m).astype(BF16), va[i, c])
                + dot(jnp.exp(far - m).astype(BF16), va[i, before])
            )
            return total / pltpu.roll(total, HD, 1)

        for i in range(heads // 2):
            pair = jnp.where(low, one(2 * i), one(2 * i + 1))
            attn[c, :, i * 128 : (i + 1) * 128] = pair.astype(BF16)

        @pl.when(c != h)
        def _():
            a_copy(c, lax.rem(h - c + n_head, n_head)).start()

    def share_w():
        for d in range(1, n_head):
            wz_copy(d).wait_recv()

        @pl.loop(1, SPLIT)
        def _(k):
            wp_copy(my_slice, lax.rem(my_slice + k, SPLIT)).start()

    @pl.loop(0, n_head + 1)
    def _(r):
        left, right = h - r, h + r
        has_left = left >= 0
        has_right = (right < n_head) & (r > 0)

        @pl.when(has_left & (r > 0))
        def _():
            x_copy(left, 1, h).wait_recv()

            @pl.when(h < n_head - 1)
            def _():
                x_copy(left, 1, h + 1).start()

        @pl.when(has_right)
        def _():
            x_copy(right, 0, h).wait_recv()

            @pl.when(h > 0)
            def _():
                x_copy(right, 0, h - 1).start()

        @pl.loop(0, 2)
        def _(j):
            @pl.when((has_left & (j == 0)) | (has_right & (j == 1)))
            def _():
                project(h + (2 * j - 1) * r)

        @pl.when(r == 1)
        def _():
            take_cache()

        @pl.when(r == 2)
        def _():
            share_w()

        @pl.loop(0, 3)
        def _(j):
            ok = has_left & (r > 0) & (j == 0)
            ok = ok | (has_right & (j == 1)) | ((r == 1) & (j == 2))

            @pl.when(ok)
            def _():
                step = jnp.where(j == 2, 0, 2 * j - 1)
                prefix(h + step * r)

        @pl.loop(0, 2)
        def _(j):
            c = jnp.where(j == 0, right, left + 1)
            ok = (has_right & (j == 0)) | ((left + 1 >= 0) & (r > 0) & (j == 1))

            @pl.when(ok)
            def _():
                finish(c)

    total = dot(attn[h], wo[...])

    @pl.loop(1, SPLIT)
    def _(k):
        owner = lax.rem(my_slice + k, SPLIT)
        wp_copy(owner, my_slice).wait_recv()

    for d in range(1, n_head):
        a_copy(h, d).wait_recv()
        total = total + dot(attn_rel[d - 1], wo_rel[d - 1])
    out[...] = total.astype(BF16)

    @pl.loop(0, n_head)
    def _(c):
        @pl.when((h > 0) & (c >= h))
        def _():
            x_copy(c, 0, h).wait_send()

        @pl.when((h < n_head - 1) & (c <= h))
        def _():
            x_copy(c, 1, h).wait_send()

        @pl.when(c != h)
        def _():
            a_copy(c, 1).wait_send()

    @pl.loop(1, half)
    def _(k):
        c_copy(cache, p, c_send.at[k], sibling).wait_send()

    @pl.loop(0, half)
    def _(k):
        c_copy(cache, p, c_fwd.at[k], sibling).wait_send()

    for d in range(1, n_head):
        wz_copy(d).wait_send()

    @pl.loop(1, SPLIT)
    def _(k):
        wp_copy(my_slice, lax.rem(my_slice + k, SPLIT)).wait_send()


def shards(
    n_head,
    n_page,
    hidden_in,
    norm_gain,
    w_qkv,
    w_out,
    cache_kv,
    page_node,
    page_fill,
    node_parent,
    tok_seg,
    req_leaf,
):
    rows, model = hidden_in.shape[1:]
    width = w_qkv.shape[2]
    heads = width // HD
    dev_pages, page_len = cache_kv.shape[1:3]
    pages = n_page * dev_pages
    vmem = pl.BlockSpec(memory_space=pltpu.VMEM)
    smem = pl.BlockSpec(memory_space=pltpu.SMEM)
    dma = pltpu.SemaphoreType.DMA
    dims = (n_head, n_page, node_parent.shape[0], req_leaf.shape[1])
    flops = 2 * n_head * rows * (4 * model * width + 4 * heads * 64 * pages * page_len)
    result = pl.pallas_call(
        functools.partial(kernel, dims),
        out_shape=jax.ShapeDtypeStruct((rows, model), BF16),
        in_specs=[vmem] * 5 + [smem] * 3 + [vmem, smem],
        out_specs=vmem,
        scratch_shapes=[
            pltpu.VMEM((n_head, rows, model), BF16),
            pltpu.VMEM((n_page,) + cache_kv.shape, BF16),
            pltpu.VMEM((n_head - 1, width, model), BF16),
            pltpu.VMEM((heads, n_head, rows, 128), BF16),
            pltpu.VMEM((heads, n_head, rows, 128), BF16),
            pltpu.VMEM((heads, n_head, rows, 128), BF16),
            pltpu.VMEM((heads, pages, page_len, 128), BF16),
            pltpu.VMEM((heads, pages, page_len, 128), BF16),
            pltpu.VMEM((heads, n_head, rows, 128), F32),
            pltpu.VMEM((heads, n_head, rows, 128), F32),
            pltpu.VMEM((n_head, rows, 128), F32),
            pltpu.VMEM((n_head, rows, 128), F32),
            pltpu.VMEM((n_head, rows, width), BF16),
            pltpu.VMEM((n_head - 1, rows, width), BF16),
            dma((2, n_head)),
            dma((n_head,)),
            dma((n_page // 2,)),
            dma((n_page // 2,)),
            dma((n_page,)),
            dma((n_head - 1,)),
            dma((n_head - 1,)),
            dma((SPLIT,)),
            dma((SPLIT,)),
            dma((n_head,)),
            dma((n_head - 1,)),
        ],
        compiler_params=pltpu.CompilerParams(
            collective_id=0, has_side_effects=True, vmem_limit_bytes=60 * 1024 * 1024
        ),
        cost_estimate=pl.CostEstimate(
            flops=flops, bytes_accessed=4 * 1024 * 1024, transcendentals=0
        ),
    )(
        hidden_in[0],
        norm_gain.reshape(1, model),
        w_qkv.reshape(model, 3 * width),
        w_out,
        cache_kv,
        page_node,
        page_fill,
        node_parent,
        tok_seg,
        req_leaf,
    )
    return result[None]


def solution(mesh):
    placed = (
        P("page", "head", None),
        P(),
        P(None, None, "head"),
        P("head", None),
        P(None, "page", None, "head"),
        P(),
        P(),
        P(),
        P("page", None),
        P("page", None),
    )
    body = functools.partial(shards, mesh.shape["head"], mesh.shape["page"])
    return jax.shard_map(
        body, mesh=mesh, in_specs=placed, out_specs=P("page", "head", None), check_vma=False
    )
```

```python
import functools

import jax
import jax.numpy as jnp
from jax import lax
from jax.experimental import pallas as pl
from jax.experimental.pallas import tpu as pltpu
from jax.sharding import PartitionSpec as P

HD = 64
EPSILON = 1e-06
BIG = 1e30
KEY_BLOCK = 2048
SPLIT = 8
MESH = pl.DeviceIdType.MESH
F32 = jnp.float32
BF16 = jnp.bfloat16


def dot_t(a, b):
    return lax.dot_general(a, b, (((1,), (1,)), ((), ())), preferred_element_type=F32)


def dot(a, b):
    return jnp.dot(a, b, preferred_element_type=F32)


def weigh(s, m):
    return jnp.exp((s - m).astype(BF16))


def kernel(
    dims,
    hid,
    gain,
    w_hbm,
    wo,
    cache,
    page_node,
    page_fill,
    parent,
    seg,
    leaf,
    out,
    normed,
    cache_all,
    wo_rel,
    qa,
    ka,
    va,
    kp,
    vp,
    acc,
    top,
    qext,
    kext,
    attn,
    attn_rel,
    w,
    w_sem,
    x_send,
    x_recv,
    c_send,
    c_fwd,
    c_recv,
    wz_send,
    wz_recv,
    wp_send,
    wp_recv,
    a_send,
    a_recv,
):
    n_head, n_page, n_nodes, n_segs = dims
    h = lax.axis_index("head")
    p = lax.axis_index("page")
    rows = hid.shape[0]
    width = w_hbm.shape[2]
    heads = width // HD
    dev_pages, page_len = cache.shape[1], cache.shape[2]
    half = n_page // 2
    sibling = p + 1 - 2 * lax.rem(p, 2)
    slice_rows = wo.shape[0] // SPLIT
    my_slice = lax.rem(p, SPLIT)
    group = p - my_slice

    w_copy = pltpu.make_async_copy(w_hbm, w, w_sem)
    w_copy.start()

    barrier = pltpu.get_barrier_semaphore()
    for d in range(1, n_head):
        pl.semaphore_signal(
            barrier, inc=1, device_id=(lax.rem(h + d, n_head), p), device_id_type=MESH
        )

    @pl.loop(1, n_page)
    def _(k):
        pl.semaphore_signal(
            barrier, inc=1, device_id=(h, lax.rem(p + k, n_page)), device_id_type=MESH
        )

    wide = hid[...].astype(F32)
    scale = lax.rsqrt(jnp.mean(wide * wide, axis=1, keepdims=True) + EPSILON)
    normed[h] = (wide * scale * gain[...]).astype(BF16)
    pl.semaphore_wait(barrier, n_head - 1 + n_page - 1)

    def x_copy(c, way, target):
        return pltpu.make_async_remote_copy(
            src_ref=normed.at[c],
            dst_ref=normed.at[c],
            send_sem=x_send.at[way, c],
            recv_sem=x_recv.at[c],
            device_id=(target, p),
            device_id_type=MESH,
        )

    def c_copy(src, slot, sem, target):
        return pltpu.make_async_remote_copy(
            src_ref=src,
            dst_ref=cache_all.at[slot],
            send_sem=sem,
            recv_sem=c_recv.at[slot],
            device_id=(h, target),
            device_id_type=MESH,
        )

    def wz_copy(d):
        part = pl.ds(pl.multiple_of(my_slice * slice_rows, slice_rows), slice_rows)
        return pltpu.make_async_remote_copy(
            src_ref=wo.at[part],
            dst_ref=wo_rel.at[d - 1, part],
            send_sem=wz_send.at[d - 1],
            recv_sem=wz_recv.at[d - 1],
            device_id=(lax.rem(h + n_head - d, n_head), p),
            device_id_type=MESH,
        )

    def wp_copy(owner, target):
        part = pl.ds(pl.multiple_of(owner * slice_rows, slice_rows), slice_rows)
        block = wo_rel.at[:, part]
        return pltpu.make_async_remote_copy(
            src_ref=block,
            dst_ref=block,
            send_sem=wp_send.at[target],
            recv_sem=wp_recv.at[owner],
            device_id=(h, group + target),
            device_id_type=MESH,
        )

    def a_copy(c, d):
        return pltpu.make_async_remote_copy(
            src_ref=attn.at[c],
            dst_ref=attn_rel.at[d - 1],
            send_sem=a_send.at[c],
            recv_sem=a_recv.at[d - 1],
            device_id=(c, p),
            device_id_type=MESH,
        )

    @pl.when(h > 0)
    def _():
        x_copy(h, 0, h - 1).start()

    @pl.when(h < n_head - 1)
    def _():
        x_copy(h, 1, h + 1).start()

    @pl.loop(1, half)
    def _(k):
        c_copy(cache, p, c_send.at[k], lax.rem(p + 2 * k, n_page)).start()

    c_copy(cache, p, c_fwd.at[0], sibling).start()
    for d in range(1, n_head):
        wz_copy(d).start()

    lane8 = lax.broadcasted_iota(jnp.int32, (n_segs, 128), 1) & (HD - 1)
    row8 = lax.broadcasted_iota(jnp.int32, (n_segs, 128), 0)
    on_path = lane8 < 0
    for s in range(n_segs):
        low = leaf[0, s]
        mid = parent[low]
        root = parent[mid]
        hit = (lane8 == low) | (lane8 == mid) | (lane8 == root)
        on_path = on_path | (hit & (row8 == s))
    own_lane = lane8 == row8 + (n_nodes + 1)
    used = lane8 < n_nodes + 1 + n_segs
    table_q = jnp.where(used & ~on_path & ~own_lane, 1.0, 0.0)
    table_k = jnp.where(own_lane, -BIG, 0.0)
    tokens = seg.shape[1]
    member = seg[...] == lax.broadcasted_iota(jnp.int32, (n_segs, tokens), 0)
    member = jnp.where(member, 1.0, 0.0)
    turned = (((0,), (0,)), ((), ()))
    ext = lax.dot_general(member, table_q, turned, preferred_element_type=F32)
    qext[...] = ext.reshape(qext.shape)
    ext = lax.dot_general(member, table_k, turned, preferred_element_type=F32)
    kext[...] = ext.reshape(kext.shape)

    def project(c):
        x = normed[c]
        low = lax.broadcasted_iota(jnp.int32, (rows, 128), 1) < HD
        q = dot(x, w[0]).astype(BF16).astype(F32) * HD ** (-0.5)
        k = dot(x, w[1])
        v = dot(x, w[2])
        q_more, k_more = qext[c], kext[c]
        for i in range(heads // 2):
            part = slice(i * 128, (i + 1) * 128)
            qa[2 * i, c] = jnp.where(low, q[:, part], q_more).astype(BF16)
            qa[2 * i + 1, c] = jnp.where(low, q_more, q[:, part]).astype(BF16)
            ka[2 * i, c] = jnp.where(low, k[:, part], k_more).astype(BF16)
            ka[2 * i + 1, c] = jnp.where(low, k_more, k[:, part]).astype(BF16)
            va[2 * i, c] = jnp.where(low, v[:, part], 1.0).astype(BF16)
            va[2 * i + 1, c] = jnp.where(low, 1.0, v[:, part]).astype(BF16)

    def widen_page(g, source, i):
        lane = lax.broadcasted_iota(jnp.int32, (page_len, 128), 1)
        low, slot = lane < HD, lax.broadcasted_iota(jnp.int32, (page_len, 128), 0)
        lane = lane & (HD - 1)
        hidden = (lane == page_node[g]) | ((lane == n_nodes) & (slot >= page_fill[g]))
        more = jnp.where(hidden, -BIG, 0.0)
        for j in range(heads // 2):
            part = slice(j * 128, (j + 1) * 128)
            k = cache_all[source, 0, i, :, part].astype(F32)
            v = cache_all[source, 1, i, :, part].astype(F32)
            kp[2 * j, g] = jnp.where(low, k, more).astype(BF16)
            kp[2 * j + 1, g] = jnp.where(low, more, k).astype(BF16)
            vp[2 * j, g] = jnp.where(low, v, 1.0).astype(BF16)
            vp[2 * j + 1, g] = jnp.where(low, 1.0, v).astype(BF16)

    def take_cache():
        @pl.loop(1, half)
        def _(k):
            source = lax.rem(p + 2 * k, n_page)
            c_copy(cache, source, c_send.at[k], sibling).wait_recv()
            c_copy(cache_all.at[source], source, c_fwd.at[k], sibling).start()

        @pl.loop(0, half)
        def _(k):
            source = lax.rem(sibling + 2 * k, n_page)
            c_copy(cache, source, c_fwd.at[0], sibling).wait_recv()

        cache_all[p] = cache[...]

        @pl.loop(0, n_page)
        def _(source):
            for i in range(dev_pages):
                widen_page(source * dev_pages + i, source, i)

    n_keys = n_page * dev_pages * page_len
    block = min(KEY_BLOCK, n_keys)
    block_pages = block // page_len
    blocks = n_keys // block

    def prefix_head(c, i):
        q = qa[i, c]

        def scores(b):
            at = pl.ds(b * block_pages, block_pages)
            s = dot_t(q, kp[i, at].reshape(block, 128))
            return s, vp[i, at].reshape(block, 128)

        s, v = scores(0)
        m = jnp.max(s, axis=1, keepdims=True)
        acc[i, c] = dot(weigh(s, m), v)
        top[i, c] = jnp.broadcast_to(m, (rows, 128))
        if blocks > 1:

            @pl.loop(1, blocks)
            def _(b):
                s, v = scores(b)
                old = top[i, c][:, :1]
                m = jnp.maximum(old, jnp.max(s, axis=1, keepdims=True))
                acc[i, c] = acc[i, c] * jnp.exp(old - m) + dot(weigh(s, m), v)
                top[i, c] = jnp.broadcast_to(m, (rows, 128))

    def prefix(c):
        @pl.loop(0, heads // 2)
        def _(pair):
            for i in (2 * pair, 2 * pair + 1):
                prefix_head(c, i)

    def finish(c):
        before = jnp.maximum(c - 1, 0)
        shut = jnp.where(c > 0, 0.0, -BIG)
        low = lax.broadcasted_iota(jnp.int32, (rows, 128), 1) < HD
        at = lax.broadcasted_iota(jnp.int32, (rows, rows), 0)
        seen = lax.broadcasted_iota(jnp.int32, (rows, rows), 1) <= at

        def one(i):
            q = qa[i, c]
            near = jnp.where(seen, dot_t(q, ka[i, c]), -BIG)
            far = dot_t(q, ka[i, before]) + shut
            old = top[i, c][:, :1]
            m = jnp.maximum(old, jnp.max(jnp.maximum(near, far), axis=1, keepdims=True))
            total = (
                acc[i, c] * jnp.exp(old - m)
                + dot(weigh(near, m), va[i, c])
                + dot(weigh(far, m), va[i, before])
            )
            return total / pltpu.roll(total, HD, 1)

        for i in range(heads // 2):
            pair = jnp.where(low, one(2 * i), one(2 * i + 1))
            attn[c, :, i * 128 : (i + 1) * 128] = pair.astype(BF16)

        @pl.when(c != h)
        def _():
            a_copy(c, lax.rem(h - c + n_head, n_head)).start()

    def share_w():
        for d in range(1, n_head):
            wz_copy(d).wait_recv()

        @pl.loop(1, SPLIT)
        def _(k):
            wp_copy(my_slice, lax.rem(my_slice + k, SPLIT)).start()

    w_copy.wait()

    @pl.loop(0, n_head)
    def _(r):
        left, right = h - r, h + r
        has_left = left >= 0
        has_right = (right < n_head) & (r > 0)

        @pl.when(has_left & (r > 0))
        def _():
            x_copy(left, 1, h).wait_recv()

            @pl.when(h < n_head - 1)
            def _():
                x_copy(left, 1, h + 1).start()

        @pl.when(has_right)
        def _():
            x_copy(right, 0, h).wait_recv()

            @pl.when(h > 0)
            def _():
                x_copy(right, 0, h - 1).start()

        @pl.loop(0, 2)
        def _(j):
            @pl.when((has_left & (j == 0)) | (has_right & (j == 1)))
            def _():
                project(h + (2 * j - 1) * r)

        @pl.when(r == 1)
        def _():
            take_cache()

        @pl.when(r == 2)
        def _():
            share_w()

        @pl.loop(0, 4)
        def _(j):
            side = 2 * (j & 1) - 1
            far = jnp.where(r == 1, 0, jnp.where(j < 2, r - 1, r))
            c = h + side * far
            ok = ((r == 1) & (j == 0)) | ((r == 2) & (c >= 0) & (c < n_head))
            ok = ok | ((r > 2) & (j >= 2) & (c >= 0) & (c < n_head))

            @pl.when(ok)
            def _():
                prefix(c)

            ripe = ok & ((j != 2) | (c == 0))
            ripe = ripe | ((r > 2) & (j == 0) & (c > 0))

            @pl.when(ripe)
            def _():
                finish(c)

    total = dot(attn[h], wo[...])

    @pl.loop(1, SPLIT)
    def _(k):
        owner = lax.rem(my_slice + k, SPLIT)
        wp_copy(owner, my_slice).wait_recv()

    for d in range(1, n_head):
        a_copy(h, d).wait_recv()
        total = total + dot(attn_rel[d - 1], wo_rel[d - 1])
    out[...] = total.astype(BF16)

    @pl.loop(0, n_head)
    def _(c):
        @pl.when((h > 0) & (c >= h))
        def _():
            x_copy(c, 0, h).wait_send()

        @pl.when((h < n_head - 1) & (c <= h))
        def _():
            x_copy(c, 1, h).wait_send()

        @pl.when(c != h)
        def _():
            a_copy(c, 1).wait_send()

    @pl.loop(1, half)
    def _(k):
        c_copy(cache, p, c_send.at[k], sibling).wait_send()

    @pl.loop(0, half)
    def _(k):
        c_copy(cache, p, c_fwd.at[k], sibling).wait_send()

    for d in range(1, n_head):
        wz_copy(d).wait_send()

    @pl.loop(1, SPLIT)
    def _(k):
        wp_copy(my_slice, lax.rem(my_slice + k, SPLIT)).wait_send()


def shards(
    n_head,
    n_page,
    hidden_in,
    norm_gain,
    w_qkv,
    w_out,
    cache_kv,
    page_node,
    page_fill,
    node_parent,
    tok_seg,
    req_leaf,
):
    rows, model = hidden_in.shape[1:]
    width = w_qkv.shape[2]
    heads = width // HD
    dev_pages, page_len = cache_kv.shape[1:3]
    pages = n_page * dev_pages
    vmem = pl.BlockSpec(memory_space=pltpu.VMEM)
    smem = pl.BlockSpec(memory_space=pltpu.SMEM)
    dma = pltpu.SemaphoreType.DMA
    dims = (n_head, n_page, node_parent.shape[0], req_leaf.shape[1])
    flops = 2 * n_head * rows * (4 * model * width + 4 * heads * 64 * pages * page_len)
    result = pl.pallas_call(
        functools.partial(kernel, dims),
        out_shape=jax.ShapeDtypeStruct((rows, model), BF16),
        in_specs=[vmem] * 2 + [pl.BlockSpec(memory_space=pl.ANY)] + [vmem] * 2 + [smem] * 3 + [vmem, smem],
        out_specs=vmem,
        scratch_shapes=[
            pltpu.VMEM((n_head, rows, model), BF16),
            pltpu.VMEM((n_page,) + cache_kv.shape, BF16),
            pltpu.VMEM((n_head - 1, width, model), BF16),
            pltpu.VMEM((heads, n_head, rows, 128), BF16),
            pltpu.VMEM((heads, n_head, rows, 128), BF16),
            pltpu.VMEM((heads, n_head, rows, 128), BF16),
            pltpu.VMEM((heads, pages, page_len, 128), BF16),
            pltpu.VMEM((heads, pages, page_len, 128), BF16),
            pltpu.VMEM((heads, n_head, rows, 128), F32),
            pltpu.VMEM((heads, n_head, rows, 128), F32),
            pltpu.VMEM((n_head, rows, 128), F32),
            pltpu.VMEM((n_head, rows, 128), F32),
            pltpu.VMEM((n_head, rows, width), BF16),
            pltpu.VMEM((n_head - 1, rows, width), BF16),
            pltpu.VMEM((3, model, width), BF16),
            dma,
            dma((2, n_head)),
            dma((n_head,)),
            dma((n_page // 2,)),
            dma((n_page // 2,)),
            dma((n_page,)),
            dma((n_head - 1,)),
            dma((n_head - 1,)),
            dma((SPLIT,)),
            dma((SPLIT,)),
            dma((n_head,)),
            dma((n_head - 1,)),
        ],
        compiler_params=pltpu.CompilerParams(
            collective_id=0, has_side_effects=True, vmem_limit_bytes=60 * 1024 * 1024
        ),
        cost_estimate=pl.CostEstimate(
            flops=flops, bytes_accessed=4 * 1024 * 1024, transcendentals=0
        ),
    )(
        hidden_in[0],
        norm_gain.reshape(1, model),
        jnp.transpose(w_qkv, (1, 0, 2)),
        w_out,
        cache_kv,
        page_node,
        page_fill,
        node_parent,
        tok_seg,
        req_leaf,
    )
    return result[None]


def solution(mesh):
    placed = (
        P("page", "head", None),
        P(),
        P(None, None, "head"),
        P("head", None),
        P(None, "page", None, "head"),
        P(),
        P(),
        P(),
        P("page", None),
        P("page", None),
    )
    body = functools.partial(shards, mesh.shape["head"], mesh.shape["page"])
    return jax.shard_map(
        body, mesh=mesh, in_specs=placed, out_specs=P("page", "head", None), check_vma=False
    )
```

```python
import functools

import jax
import jax.numpy as jnp
from jax import lax
from jax.experimental import pallas as pl
from jax.experimental.pallas import tpu as pltpu
from jax.sharding import PartitionSpec as P

HD = 64
EPSILON = 1e-06
BIG = 1e30
KEY_BLOCK = 2048
SPLIT = 8
MESH = pl.DeviceIdType.MESH
F32 = jnp.float32
BF16 = jnp.bfloat16


def dot_t(a, b):
    return lax.dot_general(a, b, (((1,), (1,)), ((), ())), preferred_element_type=F32)


def dot(a, b):
    return jnp.dot(a, b, preferred_element_type=F32)


def weigh(s, m):
    return jnp.exp((s - m).astype(BF16))


def kernel(
    dims,
    hid,
    gain,
    w_hbm,
    wo,
    cache,
    page_node,
    page_fill,
    parent,
    seg,
    leaf,
    out,
    normed,
    cache_all,
    wo_rel,
    qa,
    ka,
    va,
    kp,
    vp,
    acc,
    top,
    qext,
    kext,
    attn,
    attn_rel,
    w,
    w_sem,
    x_send,
    x_recv,
    c_send,
    c_fwd,
    c_recv,
    wz_send,
    wz_recv,
    wp_send,
    wp_recv,
    a_send,
    a_recv,
):
    n_head, n_page, n_nodes, n_segs = dims
    h = lax.axis_index("head")
    p = lax.axis_index("page")
    rows = hid.shape[0]
    width = w_hbm.shape[2]
    heads = width // HD
    dev_pages, page_len = cache.shape[1], cache.shape[2]
    half = n_page // 2
    pair, core = p // 2, lax.rem(p, 2)

    def chip(k):
        outer = lax.rem(pair // 2 + k // 2, half // 2)
        return 2 * outer + lax.rem(pair + k, 2)

    def chip_back(k):
        outer = lax.rem(pair // 2 + half // 2 - k // 2, half // 2)
        return 2 * outer + lax.rem(pair + k, 2)

    sibling = p + 1 - 2 * lax.rem(p, 2)
    slice_rows = wo.shape[0] // SPLIT
    my_slice = lax.rem(p, SPLIT)
    group = p - my_slice

    w_copy = pltpu.make_async_copy(w_hbm, w, w_sem)
    w_copy.start()

    barrier = pltpu.get_barrier_semaphore()
    for d in range(1, n_head):
        pl.semaphore_signal(
            barrier, inc=1, device_id=(lax.rem(h + d, n_head), p), device_id_type=MESH
        )

    @pl.loop(1, n_page)
    def _(k):
        pl.semaphore_signal(
            barrier, inc=1, device_id=(h, lax.rem(p + k, n_page)), device_id_type=MESH
        )

    wide = hid[...].astype(F32)
    scale = lax.rsqrt(jnp.mean(wide * wide, axis=1, keepdims=True) + EPSILON)
    normed[h] = (wide * scale * gain[...]).astype(BF16)
    pl.semaphore_wait(barrier, n_head - 1 + n_page - 1)

    def x_copy(c, way, target):
        return pltpu.make_async_remote_copy(
            src_ref=normed.at[c],
            dst_ref=normed.at[c],
            send_sem=x_send.at[way, c],
            recv_sem=x_recv.at[c],
            device_id=(target, p),
            device_id_type=MESH,
        )

    def c_copy(src, slot, sem, target):
        return pltpu.make_async_remote_copy(
            src_ref=src,
            dst_ref=cache_all.at[slot],
            send_sem=sem,
            recv_sem=c_recv.at[slot],
            device_id=(h, target),
            device_id_type=MESH,
        )

    def wz_copy(d):
        part = pl.ds(pl.multiple_of(my_slice * slice_rows, slice_rows), slice_rows)
        return pltpu.make_async_remote_copy(
            src_ref=wo.at[part],
            dst_ref=wo_rel.at[d - 1, part],
            send_sem=wz_send.at[d - 1],
            recv_sem=wz_recv.at[d - 1],
            device_id=(lax.rem(h + n_head - d, n_head), p),
            device_id_type=MESH,
        )

    def wp_copy(owner, target):
        part = pl.ds(pl.multiple_of(owner * slice_rows, slice_rows), slice_rows)
        block = wo_rel.at[:, part]
        return pltpu.make_async_remote_copy(
            src_ref=block,
            dst_ref=block,
            send_sem=wp_send.at[target],
            recv_sem=wp_recv.at[owner],
            device_id=(h, group + target),
            device_id_type=MESH,
        )

    def a_copy(c, d):
        return pltpu.make_async_remote_copy(
            src_ref=attn.at[c],
            dst_ref=attn_rel.at[d - 1],
            send_sem=a_send.at[c],
            recv_sem=a_recv.at[d - 1],
            device_id=(c, p),
            device_id_type=MESH,
        )

    @pl.when(h > 0)
    def _():
        x_copy(h, 0, h - 1).start()

    @pl.when(h < n_head - 1)
    def _():
        x_copy(h, 1, h + 1).start()

    @pl.loop(1, half)
    def _(k):
        c_copy(cache, p, c_send.at[k], 2 * chip_back(k) + core).start()

    c_copy(cache, p, c_fwd.at[0], sibling).start()
    for d in range(1, n_head):
        wz_copy(d).start()

    lane8 = lax.broadcasted_iota(jnp.int32, (n_segs, 128), 1) & (HD - 1)
    row8 = lax.broadcasted_iota(jnp.int32, (n_segs, 128), 0)
    on_path = lane8 < 0
    for s in range(n_segs):
        low = leaf[0, s]
        mid = parent[low]
        root = parent[mid]
        hit = (lane8 == low) | (lane8 == mid) | (lane8 == root)
        on_path = on_path | (hit & (row8 == s))
    own_lane = lane8 == row8 + (n_nodes + 1)
    used = lane8 < n_nodes + 1 + n_segs
    table_q = jnp.where(used & ~on_path & ~own_lane, 1.0, 0.0)
    table_k = jnp.where(own_lane, -BIG, 0.0)
    tokens = seg.shape[1]
    member = seg[...] == lax.broadcasted_iota(jnp.int32, (n_segs, tokens), 0)
    member = jnp.where(member, 1.0, 0.0)
    turned = (((0,), (0,)), ((), ()))
    ext = lax.dot_general(member, table_q, turned, preferred_element_type=F32)
    qext[...] = ext.reshape(qext.shape)
    ext = lax.dot_general(member, table_k, turned, preferred_element_type=F32)
    kext[...] = ext.reshape(kext.shape)

    def project(c):
        x = normed[c]
        low = lax.broadcasted_iota(jnp.int32, (rows, 128), 1) < HD
        q = dot(x, w[0]).astype(BF16).astype(F32) * HD ** (-0.5)
        k = dot(x, w[1])
        v = dot(x, w[2])
        q_more, k_more = qext[c], kext[c]
        for i in range(heads // 2):
            part = slice(i * 128, (i + 1) * 128)
            qa[2 * i, c] = jnp.where(low, q[:, part], q_more).astype(BF16)
            qa[2 * i + 1, c] = jnp.where(low, q_more, q[:, part]).astype(BF16)
            ka[2 * i, c] = jnp.where(low, k[:, part], k_more).astype(BF16)
            ka[2 * i + 1, c] = jnp.where(low, k_more, k[:, part]).astype(BF16)
            va[2 * i, c] = jnp.where(low, v[:, part], 1.0).astype(BF16)
            va[2 * i + 1, c] = jnp.where(low, 1.0, v[:, part]).astype(BF16)

    def widen_page(g, source, i):
        lane = lax.broadcasted_iota(jnp.int32, (page_len, 128), 1)
        low, slot = lane < HD, lax.broadcasted_iota(jnp.int32, (page_len, 128), 0)
        lane = lane & (HD - 1)
        hidden = (lane == page_node[g]) | ((lane == n_nodes) & (slot >= page_fill[g]))
        more = jnp.where(hidden, -BIG, 0.0)
        for j in range(heads // 2):
            part = slice(j * 128, (j + 1) * 128)
            k = cache_all[source, 0, i, :, part].astype(F32)
            v = cache_all[source, 1, i, :, part].astype(F32)
            kp[2 * j, g] = jnp.where(low, k, more).astype(BF16)
            kp[2 * j + 1, g] = jnp.where(low, more, k).astype(BF16)
            vp[2 * j, g] = jnp.where(low, v, 1.0).astype(BF16)
            vp[2 * j + 1, g] = jnp.where(low, 1.0, v).astype(BF16)

    def take_cache():
        cache_all[p] = cache[...]
        for i in range(heads):
            acc[i, h] = jnp.zeros((rows, 128), F32)
            top[i, h] = jnp.full((rows, 128), -3 * BIG, F32)

        @pl.loop(0, half)
        def _(k):
            first = 2 * chip(k)
            source, other = first + core, first + 1 - core

            @pl.when(k > 0)
            def _():
                c_copy(cache, source, c_send.at[k], sibling).wait_recv()
                c_copy(cache_all.at[source], source, c_fwd.at[k], sibling).start()

            c_copy(cache, other, c_fwd.at[0], sibling).wait_recv()
            for n in range(2):
                for i in range(dev_pages):
                    widen_page((first + n) * dev_pages + i, first + n, i)
            for i in range(heads):
                at = pl.ds(first * dev_pages, 2 * dev_pages)
                extend(h, i, at, 2 * dev_pages * page_len)

    n_keys = n_page * dev_pages * page_len
    block = min(KEY_BLOCK, n_keys)
    block_pages = block // page_len
    blocks = n_keys // block

    def extend(c, i, at, size):
        s = dot_t(qa[i, c], kp[i, at].reshape(size, 128))
        old = top[i, c][:, :1]
        m = jnp.maximum(old, jnp.max(s, axis=1, keepdims=True))
        more = dot(weigh(s, m), vp[i, at].reshape(size, 128))
        acc[i, c] = acc[i, c] * jnp.exp(old - m) + more
        top[i, c] = jnp.broadcast_to(m, (rows, 128))

    def prefix_head(c, i):
        s = dot_t(qa[i, c], kp[i, :block_pages].reshape(block, 128))
        m = jnp.max(s, axis=1, keepdims=True)
        acc[i, c] = dot(weigh(s, m), vp[i, :block_pages].reshape(block, 128))
        top[i, c] = jnp.broadcast_to(m, (rows, 128))
        if blocks > 1:

            @pl.loop(1, blocks)
            def _(b):
                extend(c, i, pl.ds(b * block_pages, block_pages), block)

    def prefix(c):
        @pl.loop(0, heads // 2)
        def _(pair):
            for i in (2 * pair, 2 * pair + 1):
                prefix_head(c, i)

    def finish(c):
        before = jnp.maximum(c - 1, 0)
        shut = jnp.where(c > 0, 0.0, -BIG)
        low = lax.broadcasted_iota(jnp.int32, (rows, 128), 1) < HD
        at = lax.broadcasted_iota(jnp.int32, (rows, rows), 0)
        seen = lax.broadcasted_iota(jnp.int32, (rows, rows), 1) <= at

        def one(i):
            q = qa[i, c]
            near = jnp.where(seen, dot_t(q, ka[i, c]), -BIG)
            far = dot_t(q, ka[i, before]) + shut
            old = top[i, c][:, :1]
            m = jnp.maximum(old, jnp.max(jnp.maximum(near, far), axis=1, keepdims=True))
            total = (
                acc[i, c] * jnp.exp(old - m)
                + dot(weigh(near, m), va[i, c])
                + dot(weigh(far, m), va[i, before])
            )
            return total / pltpu.roll(total, HD, 1)

        for i in range(heads // 2):
            pair = jnp.where(low, one(2 * i), one(2 * i + 1))
            attn[c, :, i * 128 : (i + 1) * 128] = pair.astype(BF16)

        @pl.when(c != h)
        def _():
            a_copy(c, lax.rem(h - c + n_head, n_head)).start()

    def share_w():
        for d in range(1, n_head):
            wz_copy(d).wait_recv()

        @pl.loop(1, SPLIT)
        def _(k):
            wp_copy(my_slice, lax.rem(my_slice + k, SPLIT)).start()

    w_copy.wait()

    @pl.loop(0, n_head)
    def _(r):
        left, right = h - r, h + r
        has_left = left >= 0
        has_right = (right < n_head) & (r > 0)

        @pl.when(has_left & (r > 0))
        def _():
            x_copy(left, 1, h).wait_recv()

            @pl.when(h < n_head - 1)
            def _():
                x_copy(left, 1, h + 1).start()

        @pl.when(has_right)
        def _():
            x_copy(right, 0, h).wait_recv()

            @pl.when(h > 0)
            def _():
                x_copy(right, 0, h - 1).start()

        @pl.loop(0, 2)
        def _(j):
            @pl.when((has_left & (j == 0)) | (has_right & (j == 1)))
            def _():
                project(h + (2 * j - 1) * r)

        @pl.when(r == 0)
        def _():
            take_cache()

        @pl.when(r == 2)
        def _():
            share_w()

        @pl.loop(0, 4)
        def _(j):
            c = jnp.where(j == 0, h, jnp.where(j == 1, h + r, jnp.where(j == 2, h - r + 1, h - r)))
            inside = (c >= 0) & (c < n_head) & (r > 0)
            last = h == n_head - 1
            begin = (j == 1) | ((j == 2) & (r == 2) & (h < n_head - 1))
            begin = begin | ((j == 3) & ((r > 1) | last))
            end = ((j == 0) & (r == 1)) | (j == 1)
            end = end | ((j == 2) & ((r == 2) | ((r > 2) & (c > 0))))
            end = end | ((j == 3) & (r > 1) & (c == 0))

            @pl.when(inside & begin)
            def _():
                prefix(c)

            @pl.when(inside & end)
            def _():
                finish(c)

    total = dot(attn[h], wo[...])

    @pl.loop(1, SPLIT)
    def _(k):
        owner = lax.rem(my_slice + k, SPLIT)
        wp_copy(owner, my_slice).wait_recv()

    for d in range(1, n_head):
        a_copy(h, d).wait_recv()
        total = total + dot(attn_rel[d - 1], wo_rel[d - 1])
    out[...] = total.astype(BF16)

    @pl.loop(0, n_head)
    def _(c):
        @pl.when((h > 0) & (c >= h))
        def _():
            x_copy(c, 0, h).wait_send()

        @pl.when((h < n_head - 1) & (c <= h))
        def _():
            x_copy(c, 1, h).wait_send()

        @pl.when(c != h)
        def _():
            a_copy(c, 1).wait_send()

    @pl.loop(1, half)
    def _(k):
        c_copy(cache, p, c_send.at[k], sibling).wait_send()

    @pl.loop(0, half)
    def _(k):
        c_copy(cache, p, c_fwd.at[k], sibling).wait_send()

    for d in range(1, n_head):
        wz_copy(d).wait_send()

    @pl.loop(1, SPLIT)
    def _(k):
        wp_copy(my_slice, lax.rem(my_slice + k, SPLIT)).wait_send()


def shards(
    n_head,
    n_page,
    hidden_in,
    norm_gain,
    w_qkv,
    w_out,
    cache_kv,
    page_node,
    page_fill,
    node_parent,
    tok_seg,
    req_leaf,
):
    rows, model = hidden_in.shape[1:]
    width = w_qkv.shape[2]
    heads = width // HD
    dev_pages, page_len = cache_kv.shape[1:3]
    pages = n_page * dev_pages
    vmem = pl.BlockSpec(memory_space=pltpu.VMEM)
    smem = pl.BlockSpec(memory_space=pltpu.SMEM)
    dma = pltpu.SemaphoreType.DMA
    dims = (n_head, n_page, node_parent.shape[0], req_leaf.shape[1])
    flops = 2 * n_head * rows * (4 * model * width + 4 * heads * 64 * pages * page_len)
    result = pl.pallas_call(
        functools.partial(kernel, dims),
        out_shape=jax.ShapeDtypeStruct((rows, model), BF16),
        in_specs=[vmem] * 2 + [pl.BlockSpec(memory_space=pl.ANY)] + [vmem] * 2 + [smem] * 3 + [vmem, smem],
        out_specs=vmem,
        scratch_shapes=[
            pltpu.VMEM((n_head, rows, model), BF16),
            pltpu.VMEM((n_page,) + cache_kv.shape, BF16),
            pltpu.VMEM((n_head - 1, width, model), BF16),
            pltpu.VMEM((heads, n_head, rows, 128), BF16),
            pltpu.VMEM((heads, n_head, rows, 128), BF16),
            pltpu.VMEM((heads, n_head, rows, 128), BF16),
            pltpu.VMEM((heads, pages, page_len, 128), BF16),
            pltpu.VMEM((heads, pages, page_len, 128), BF16),
            pltpu.VMEM((heads, n_head, rows, 128), F32),
            pltpu.VMEM((heads, n_head, rows, 128), F32),
            pltpu.VMEM((n_head, rows, 128), F32),
            pltpu.VMEM((n_head, rows, 128), F32),
            pltpu.VMEM((n_head, rows, width), BF16),
            pltpu.VMEM((n_head - 1, rows, width), BF16),
            pltpu.VMEM((3, model, width), BF16),
            dma,
            dma((2, n_head)),
            dma((n_head,)),
            dma((n_page // 2,)),
            dma((n_page // 2,)),
            dma((n_page,)),
            dma((n_head - 1,)),
            dma((n_head - 1,)),
            dma((SPLIT,)),
            dma((SPLIT,)),
            dma((n_head,)),
            dma((n_head - 1,)),
        ],
        compiler_params=pltpu.CompilerParams(
            collective_id=0, has_side_effects=True, vmem_limit_bytes=60 * 1024 * 1024
        ),
        cost_estimate=pl.CostEstimate(
            flops=flops, bytes_accessed=4 * 1024 * 1024, transcendentals=0
        ),
    )(
        hidden_in[0],
        norm_gain.reshape(1, model),
        jnp.transpose(w_qkv, (1, 0, 2)),
        w_out,
        cache_kv,
        page_node,
        page_fill,
        node_parent,
        tok_seg,
        req_leaf,
    )
    return result[None]


def solution(mesh):
    placed = (
        P("page", "head", None),
        P(),
        P(None, None, "head"),
        P("head", None),
        P(None, "page", None, "head"),
        P(),
        P(),
        P(),
        P("page", None),
        P("page", None),
    )
    body = functools.partial(shards, mesh.shape["head"], mesh.shape["page"])
    return jax.shard_map(
        body, mesh=mesh, in_specs=placed, out_specs=P("page", "head", None), check_vma=False
    )
```

```python
import functools

import jax
import jax.numpy as jnp
from jax import lax
from jax.experimental import pallas as pl
from jax.experimental.pallas import tpu as pltpu
from jax.sharding import PartitionSpec as P

HD = 64
EPSILON = 1e-06
BIG = 1e30
KEY_BLOCK = 2048
SPLIT = 8
MESH = pl.DeviceIdType.MESH
F32 = jnp.float32
BF16 = jnp.bfloat16


def dot_t(a, b):
    return lax.dot_general(a, b, (((1,), (1,)), ((), ())), preferred_element_type=F32)


def dot(a, b):
    return jnp.dot(a, b, preferred_element_type=F32)


def weigh(s, m):
    return jnp.exp((s - m).astype(BF16))


def kernel(
    dims,
    hid,
    gain,
    w_hbm,
    wo,
    cache,
    page_node,
    page_fill,
    parent,
    seg,
    leaf,
    out,
    normed,
    cache_all,
    wo_rel,
    qa,
    ka,
    va,
    kp,
    vp,
    acc,
    top,
    qext,
    kext,
    attn,
    attn_rel,
    w,
    w_sem,
    x_send,
    x_recv,
    c_send,
    c_fwd,
    c_recv,
    wz_send,
    wz_recv,
    wp_send,
    wp_recv,
    a_send,
    a_recv,
):
    n_head, n_page, n_nodes, n_segs = dims
    h = lax.axis_index("head")
    p = lax.axis_index("page")
    rows = hid.shape[0]
    width = w_hbm.shape[2]
    heads = width // HD
    dev_pages, page_len = cache.shape[1], cache.shape[2]
    half = n_page // 2
    pair, core = p // 2, lax.rem(p, 2)

    def chip(k):
        outer = lax.rem(pair // 2 + k // 2, half // 2)
        return 2 * outer + lax.rem(pair + k, 2)

    def chip_back(k):
        outer = lax.rem(pair // 2 + half // 2 - k // 2, half // 2)
        return 2 * outer + lax.rem(pair + k, 2)

    sibling = p + 1 - 2 * lax.rem(p, 2)
    slice_rows = wo.shape[0] // SPLIT
    my_slice = lax.rem(p, SPLIT)
    group = p - my_slice

    w_copy = pltpu.make_async_copy(w_hbm, w, w_sem)
    w_copy.start()

    barrier = pltpu.get_barrier_semaphore()
    for d in range(1, n_head):
        pl.semaphore_signal(
            barrier, inc=1, device_id=(lax.rem(h + d, n_head), p), device_id_type=MESH
        )

    @pl.loop(1, n_page)
    def _(k):
        pl.semaphore_signal(
            barrier, inc=1, device_id=(h, lax.rem(p + k, n_page)), device_id_type=MESH
        )

    wide = hid[...].astype(F32)
    scale = lax.rsqrt(jnp.mean(wide * wide, axis=1, keepdims=True) + EPSILON)
    normed[h] = (wide * scale * gain[...]).astype(BF16)
    pl.semaphore_wait(barrier, n_head - 1 + n_page - 1)

    def x_copy(c, way, target):
        return pltpu.make_async_remote_copy(
            src_ref=normed.at[c],
            dst_ref=normed.at[c],
            send_sem=x_send.at[way, c],
            recv_sem=x_recv.at[c],
            device_id=(target, p),
            device_id_type=MESH,
        )

    def c_copy(src, slot, sem, target):
        return pltpu.make_async_remote_copy(
            src_ref=src,
            dst_ref=cache_all.at[slot],
            send_sem=sem,
            recv_sem=c_recv.at[slot],
            device_id=(h, target),
            device_id_type=MESH,
        )

    def wz_copy(d):
        part = pl.ds(pl.multiple_of(my_slice * slice_rows, slice_rows), slice_rows)
        return pltpu.make_async_remote_copy(
            src_ref=wo.at[part],
            dst_ref=wo_rel.at[d - 1, part],
            send_sem=wz_send.at[d - 1],
            recv_sem=wz_recv.at[d - 1],
            device_id=(lax.rem(h + n_head - d, n_head), p),
            device_id_type=MESH,
        )

    def wp_copy(owner, target):
        part = pl.ds(pl.multiple_of(owner * slice_rows, slice_rows), slice_rows)
        block = wo_rel.at[:, part]
        return pltpu.make_async_remote_copy(
            src_ref=block,
            dst_ref=block,
            send_sem=wp_send.at[target],
            recv_sem=wp_recv.at[owner],
            device_id=(h, group + target),
            device_id_type=MESH,
        )

    def a_copy(c, d):
        return pltpu.make_async_remote_copy(
            src_ref=attn.at[c],
            dst_ref=attn_rel.at[d - 1],
            send_sem=a_send.at[c],
            recv_sem=a_recv.at[d - 1],
            device_id=(c, p),
            device_id_type=MESH,
        )

    @pl.when(h > 0)
    def _():
        x_copy(h, 0, h - 1).start()

    @pl.when(h < n_head - 1)
    def _():
        x_copy(h, 1, h + 1).start()

    @pl.loop(1, half)
    def _(k):
        c_copy(cache, p, c_send.at[k], 2 * chip_back(k) + core).start()

    c_copy(cache, p, c_fwd.at[0], sibling).start()
    for d in range(1, n_head):
        wz_copy(d).start()

    lane8 = lax.broadcasted_iota(jnp.int32, (n_segs, 128), 1) & (HD - 1)
    row8 = lax.broadcasted_iota(jnp.int32, (n_segs, 128), 0)
    on_path = lane8 < 0
    for s in range(n_segs):
        low = leaf[0, s]
        mid = parent[low]
        root = parent[mid]
        hit = (lane8 == low) | (lane8 == mid) | (lane8 == root)
        on_path = on_path | (hit & (row8 == s))
    own_lane = lane8 == row8 + (n_nodes + 1)
    used = lane8 < n_nodes + 1 + n_segs
    table_q = jnp.where(used & ~on_path & ~own_lane, 1.0, 0.0)
    table_k = jnp.where(own_lane, -BIG, 0.0)
    tokens = seg.shape[1]
    member = seg[...] == lax.broadcasted_iota(jnp.int32, (n_segs, tokens), 0)
    member = jnp.where(member, 1.0, 0.0)
    turned = (((0,), (0,)), ((), ()))
    ext = lax.dot_general(member, table_q, turned, preferred_element_type=F32)
    qext[...] = ext.reshape(qext.shape)
    ext = lax.dot_general(member, table_k, turned, preferred_element_type=F32)
    kext[...] = ext.reshape(kext.shape)

    def project(c):
        x = normed[c]
        low = lax.broadcasted_iota(jnp.int32, (rows, 128), 1) < HD
        q = dot(x, w[0]).astype(BF16).astype(F32) * HD ** (-0.5)
        k = dot(x, w[1])
        v = dot(x, w[2])
        q_more, k_more = qext[c], kext[c]
        for i in range(heads // 2):
            part = slice(i * 128, (i + 1) * 128)
            qa[2 * i, c] = jnp.where(low, q[:, part], q_more).astype(BF16)
            qa[2 * i + 1, c] = jnp.where(low, q_more, q[:, part]).astype(BF16)
            ka[2 * i, c] = jnp.where(low, k[:, part], k_more).astype(BF16)
            ka[2 * i + 1, c] = jnp.where(low, k_more, k[:, part]).astype(BF16)
            va[2 * i, c] = jnp.where(low, v[:, part], 1.0).astype(BF16)
            va[2 * i + 1, c] = jnp.where(low, 1.0, v[:, part]).astype(BF16)

    def widen_page(g, source, i):
        lane = lax.broadcasted_iota(jnp.int32, (page_len, 128), 1)
        low, slot = lane < HD, lax.broadcasted_iota(jnp.int32, (page_len, 128), 0)
        lane = lane & (HD - 1)
        hidden = (lane == page_node[g]) | ((lane == n_nodes) & (slot >= page_fill[g]))
        more = jnp.where(hidden, -BIG, 0.0)
        at = pl.ds(pl.multiple_of(g * page_len, page_len), page_len)
        for j in range(heads // 2):
            part = slice(j * 128, (j + 1) * 128)
            k = cache_all[source, 0, i, :, part].astype(F32)
            v = cache_all[source, 1, i, :, part].astype(F32)
            kp[2 * j, :, at] = jnp.where(low, k, more).T.astype(BF16)
            kp[2 * j + 1, :, at] = jnp.where(low, more, k).T.astype(BF16)
            vp[2 * j, g] = jnp.where(low, v, 1.0).astype(BF16)
            vp[2 * j + 1, g] = jnp.where(low, 1.0, v).astype(BF16)

    def take_cache():
        cache_all[p] = cache[...]

        @pl.loop(0, half)
        def _(k):
            first = 2 * chip(k)
            source, other = first + core, first + 1 - core

            @pl.when(k > 0)
            def _():
                c_copy(cache, source, c_send.at[k], sibling).wait_recv()
                c_copy(cache_all.at[source], source, c_fwd.at[k], sibling).start()

            c_copy(cache, other, c_fwd.at[0], sibling).wait_recv()
            for n in range(2):
                for i in range(dev_pages):
                    widen_page((first + n) * dev_pages + i, first + n, i)

    n_keys = n_page * dev_pages * page_len
    block = min(KEY_BLOCK, n_keys)
    block_pages = block // page_len
    blocks = n_keys // block

    def prefix_head(c, i):
        s = dot(qa[i, c], kp[i, :, :block])
        m = jnp.max(s, axis=1, keepdims=True)
        acc[i, c] = dot(weigh(s, m), vp[i, :block_pages].reshape(block, 128))
        top[i, c] = jnp.broadcast_to(m, (rows, 128))
        if blocks > 1:

            @pl.loop(1, blocks)
            def _(b):
                s = dot(qa[i, c], kp[i, :, pl.ds(pl.multiple_of(b * block, block), block)])
                old = top[i, c][:, :1]
                m = jnp.maximum(old, jnp.max(s, axis=1, keepdims=True))
                v = vp[i, pl.ds(b * block_pages, block_pages)].reshape(block, 128)
                acc[i, c] = acc[i, c] * jnp.exp(old - m) + dot(weigh(s, m), v)
                top[i, c] = jnp.broadcast_to(m, (rows, 128))

    def prefix(c):
        @pl.loop(0, heads // 2)
        def _(pair):
            for i in (2 * pair, 2 * pair + 1):
                prefix_head(c, i)

    def finish(c):
        before = jnp.maximum(c - 1, 0)
        shut = jnp.where(c > 0, 0.0, -BIG)
        low = lax.broadcasted_iota(jnp.int32, (rows, 128), 1) < HD
        at = lax.broadcasted_iota(jnp.int32, (rows, rows), 0)
        seen = lax.broadcasted_iota(jnp.int32, (rows, rows), 1) <= at

        def one(i):
            q = qa[i, c]
            near = jnp.where(seen, dot_t(q, ka[i, c]), -BIG)
            far = dot_t(q, ka[i, before]) + shut
            old = top[i, c][:, :1]
            m = jnp.maximum(old, jnp.max(jnp.maximum(near, far), axis=1, keepdims=True))
            total = (
                acc[i, c] * jnp.exp(old - m)
                + dot(weigh(near, m), va[i, c])
                + dot(weigh(far, m), va[i, before])
            )
            return total / pltpu.roll(total, HD, 1)

        for i in range(heads // 2):
            pair = jnp.where(low, one(2 * i), one(2 * i + 1))
            attn[c, :, i * 128 : (i + 1) * 128] = pair.astype(BF16)

        @pl.when(c != h)
        def _():
            a_copy(c, lax.rem(h - c + n_head, n_head)).start()

    def share_w():
        for d in range(1, n_head):
            wz_copy(d).wait_recv()

        @pl.loop(1, SPLIT)
        def _(k):
            wp_copy(my_slice, lax.rem(my_slice + k, SPLIT)).start()

    w_copy.wait()

    @pl.loop(0, n_head)
    def _(r):
        left, right = h - r, h + r
        has_left = left >= 0
        has_right = (right < n_head) & (r > 0)

        @pl.when(has_left & (r > 0))
        def _():
            x_copy(left, 1, h).wait_recv()

            @pl.when(h < n_head - 1)
            def _():
                x_copy(left, 1, h + 1).start()

        @pl.when(has_right)
        def _():
            x_copy(right, 0, h).wait_recv()

            @pl.when(h > 0)
            def _():
                x_copy(right, 0, h - 1).start()

        @pl.loop(0, 2)
        def _(j):
            @pl.when((has_left & (j == 0)) | (has_right & (j == 1)))
            def _():
                project(h + (2 * j - 1) * r)

        @pl.when(r == 0)
        def _():
            take_cache()

        @pl.when(r == 2)
        def _():
            share_w()

        @pl.loop(0, 4)
        def _(j):
            side = 2 * (j & 1) - 1
            far = jnp.where(r == 1, 0, jnp.where(j < 2, r - 1, r))
            c = h + side * far
            ok = ((r == 1) & (j == 0)) | ((r == 2) & (c >= 0) & (c < n_head))
            ok = ok | ((r > 2) & (j >= 2) & (c >= 0) & (c < n_head))

            @pl.when(ok)
            def _():
                prefix(c)

            ripe = ok & ((j != 2) | (c == 0))
            ripe = ripe | ((r > 2) & (j == 0) & (c > 0))

            @pl.when(ripe)
            def _():
                finish(c)

    total = dot(attn[h], wo[...])

    @pl.loop(1, SPLIT)
    def _(k):
        owner = lax.rem(my_slice + k, SPLIT)
        wp_copy(owner, my_slice).wait_recv()

    for d in range(1, n_head):
        a_copy(h, d).wait_recv()
        total = total + dot(attn_rel[d - 1], wo_rel[d - 1])
    out[...] = total.astype(BF16)

    @pl.loop(0, n_head)
    def _(c):
        @pl.when((h > 0) & (c >= h))
        def _():
            x_copy(c, 0, h).wait_send()

        @pl.when((h < n_head - 1) & (c <= h))
        def _():
            x_copy(c, 1, h).wait_send()

        @pl.when(c != h)
        def _():
            a_copy(c, 1).wait_send()

    @pl.loop(1, half)
    def _(k):
        c_copy(cache, p, c_send.at[k], sibling).wait_send()

    @pl.loop(0, half)
    def _(k):
        c_copy(cache, p, c_fwd.at[k], sibling).wait_send()

    for d in range(1, n_head):
        wz_copy(d).wait_send()

    @pl.loop(1, SPLIT)
    def _(k):
        wp_copy(my_slice, lax.rem(my_slice + k, SPLIT)).wait_send()


def shards(
    n_head,
    n_page,
    hidden_in,
    norm_gain,
    w_qkv,
    w_out,
    cache_kv,
    page_node,
    page_fill,
    node_parent,
    tok_seg,
    req_leaf,
):
    rows, model = hidden_in.shape[1:]
    width = w_qkv.shape[2]
    heads = width // HD
    dev_pages, page_len = cache_kv.shape[1:3]
    pages = n_page * dev_pages
    vmem = pl.BlockSpec(memory_space=pltpu.VMEM)
    smem = pl.BlockSpec(memory_space=pltpu.SMEM)
    dma = pltpu.SemaphoreType.DMA
    dims = (n_head, n_page, node_parent.shape[0], req_leaf.shape[1])
    flops = 2 * n_head * rows * (4 * model * width + 4 * heads * 64 * pages * page_len)
    result = pl.pallas_call(
        functools.partial(kernel, dims),
        out_shape=jax.ShapeDtypeStruct((rows, model), BF16),
        in_specs=[vmem] * 2 + [pl.BlockSpec(memory_space=pl.ANY)] + [vmem] * 2 + [smem] * 3 + [vmem, smem],
        out_specs=vmem,
        scratch_shapes=[
            pltpu.VMEM((n_head, rows, model), BF16),
            pltpu.VMEM((n_page,) + cache_kv.shape, BF16),
            pltpu.VMEM((n_head - 1, width, model), BF16),
            pltpu.VMEM((heads, n_head, rows, 128), BF16),
            pltpu.VMEM((heads, n_head, rows, 128), BF16),
            pltpu.VMEM((heads, n_head, rows, 128), BF16),
            pltpu.VMEM((heads, 128, pages * page_len), BF16),
            pltpu.VMEM((heads, pages, page_len, 128), BF16),
            pltpu.VMEM((heads, n_head, rows, 128), F32),
            pltpu.VMEM((heads, n_head, rows, 128), F32),
            pltpu.VMEM((n_head, rows, 128), F32),
            pltpu.VMEM((n_head, rows, 128), F32),
            pltpu.VMEM((n_head, rows, width), BF16),
            pltpu.VMEM((n_head - 1, rows, width), BF16),
            pltpu.VMEM((3, model, width), BF16),
            dma,
            dma((2, n_head)),
            dma((n_head,)),
            dma((n_page // 2,)),
            dma((n_page // 2,)),
            dma((n_page,)),
            dma((n_head - 1,)),
            dma((n_head - 1,)),
            dma((SPLIT,)),
            dma((SPLIT,)),
            dma((n_head,)),
            dma((n_head - 1,)),
        ],
        compiler_params=pltpu.CompilerParams(
            collective_id=0, has_side_effects=True, vmem_limit_bytes=60 * 1024 * 1024
        ),
        cost_estimate=pl.CostEstimate(
            flops=flops, bytes_accessed=4 * 1024 * 1024, transcendentals=0
        ),
    )(
        hidden_in[0],
        norm_gain.reshape(1, model),
        jnp.transpose(w_qkv, (1, 0, 2)),
        w_out,
        cache_kv,
        page_node,
        page_fill,
        node_parent,
        tok_seg,
        req_leaf,
    )
    return result[None]


def solution(mesh):
    placed = (
        P("page", "head", None),
        P(),
        P(None, None, "head"),
        P("head", None),
        P(None, "page", None, "head"),
        P(),
        P(),
        P(),
        P("page", None),
        P("page", None),
    )
    body = functools.partial(shards, mesh.shape["head"], mesh.shape["page"])
    return jax.shard_map(
        body, mesh=mesh, in_specs=placed, out_specs=P("page", "head", None), check_vma=False
    )
```

```python
import functools

import jax
import jax.numpy as jnp
from jax import lax
from jax.experimental import pallas as pl
from jax.experimental.pallas import tpu as pltpu
from jax.sharding import PartitionSpec as P

HD = 64
EPSILON = 1e-06
BIG = 1e30
KEY_BLOCK = 2048
SPLIT = 8
MESH = pl.DeviceIdType.MESH
F32 = jnp.float32
BF16 = jnp.bfloat16


def dot_t(a, b):
    return lax.dot_general(a, b, (((1,), (1,)), ((), ())), preferred_element_type=F32)


def dot(a, b):
    return jnp.dot(a, b, preferred_element_type=F32)


def weigh(s, m):
    return jnp.exp((s - m).astype(BF16))


def kernel(
    dims,
    hid,
    gain,
    w_hbm,
    wo,
    cache,
    page_node,
    page_fill,
    parent,
    seg,
    leaf,
    out,
    normed,
    cache_all,
    wo_rel,
    qa,
    ka,
    va,
    kp,
    vp,
    acc,
    top,
    qext,
    kext,
    attn,
    attn_rel,
    w,
    w_sem,
    x_send,
    x_recv,
    c_send,
    c_fwd,
    c_recv,
    wz_send,
    wz_recv,
    wp_send,
    wp_recv,
    a_send,
    a_recv,
):
    n_head, n_page, n_nodes, n_segs = dims
    h = lax.axis_index("head")
    p = lax.axis_index("page")
    rows = hid.shape[0]
    width = w_hbm.shape[2]
    heads = width // HD
    dev_pages, page_len = cache.shape[1], cache.shape[2]
    half = n_page // 2
    pair, core = p // 2, lax.rem(p, 2)

    def chip(k):
        outer = lax.rem(pair // 2 + k // 2, half // 2)
        return 2 * outer + lax.rem(pair + k, 2)

    def chip_back(k):
        outer = lax.rem(pair // 2 + half // 2 - k // 2, half // 2)
        return 2 * outer + lax.rem(pair + k, 2)

    sibling = p + 1 - 2 * lax.rem(p, 2)
    slice_rows = wo.shape[0] // SPLIT
    my_slice = lax.rem(p, SPLIT)
    group = p - my_slice

    w_copy = pltpu.make_async_copy(w_hbm, w, w_sem)
    w_copy.start()

    barrier = pltpu.get_barrier_semaphore()
    for d in range(1, n_head):
        pl.semaphore_signal(
            barrier, inc=1, device_id=(lax.rem(h + d, n_head), p), device_id_type=MESH
        )

    @pl.loop(1, n_page)
    def _(k):
        pl.semaphore_signal(
            barrier, inc=1, device_id=(h, lax.rem(p + k, n_page)), device_id_type=MESH
        )

    wide = hid[...].astype(F32)
    scale = lax.rsqrt(jnp.mean(wide * wide, axis=1, keepdims=True) + EPSILON)
    normed[h] = (wide * scale * gain[...]).astype(BF16)
    pl.semaphore_wait(barrier, n_head - 1 + n_page - 1)

    def x_copy(c, way, target):
        return pltpu.make_async_remote_copy(
            src_ref=normed.at[c],
            dst_ref=normed.at[c],
            send_sem=x_send.at[way, c],
            recv_sem=x_recv.at[c],
            device_id=(target, p),
            device_id_type=MESH,
        )

    def c_copy(src, slot, sem, target):
        return pltpu.make_async_remote_copy(
            src_ref=src,
            dst_ref=cache_all.at[slot],
            send_sem=sem,
            recv_sem=c_recv.at[slot],
            device_id=(h, target),
            device_id_type=MESH,
        )

    def wz_copy(d):
        part = pl.ds(pl.multiple_of(my_slice * slice_rows, slice_rows), slice_rows)
        return pltpu.make_async_remote_copy(
            src_ref=wo.at[part],
            dst_ref=wo_rel.at[d - 1, part],
            send_sem=wz_send.at[d - 1],
            recv_sem=wz_recv.at[d - 1],
            device_id=(lax.rem(h + n_head - d, n_head), p),
            device_id_type=MESH,
        )

    def wp_copy(owner, target):
        part = pl.ds(pl.multiple_of(owner * slice_rows, slice_rows), slice_rows)
        block = wo_rel.at[:, part]
        return pltpu.make_async_remote_copy(
            src_ref=block,
            dst_ref=block,
            send_sem=wp_send.at[target],
            recv_sem=wp_recv.at[owner],
            device_id=(h, group + target),
            device_id_type=MESH,
        )

    def a_copy(c, d):
        return pltpu.make_async_remote_copy(
            src_ref=attn.at[c],
            dst_ref=attn_rel.at[d - 1],
            send_sem=a_send.at[c],
            recv_sem=a_recv.at[d - 1],
            device_id=(c, p),
            device_id_type=MESH,
        )

    @pl.when(h > 0)
    def _():
        x_copy(h, 0, h - 1).start()

    @pl.when(h < n_head - 1)
    def _():
        x_copy(h, 1, h + 1).start()

    @pl.loop(1, half)
    def _(k):
        c_copy(cache, p, c_send.at[k], 2 * chip_back(k) + core).start()

    c_copy(cache, p, c_fwd.at[0], sibling).start()
    for d in range(1, n_head):
        wz_copy(d).start()

    lane8 = lax.broadcasted_iota(jnp.int32, (n_segs, 128), 1) & (HD - 1)
    row8 = lax.broadcasted_iota(jnp.int32, (n_segs, 128), 0)
    on_path = lane8 < 0
    for s in range(n_segs):
        low = leaf[0, s]
        mid = parent[low]
        root = parent[mid]
        hit = (lane8 == low) | (lane8 == mid) | (lane8 == root)
        on_path = on_path | (hit & (row8 == s))
    own_lane = lane8 == row8 + (n_nodes + 1)
    used = lane8 < n_nodes + 1 + n_segs
    table_q = jnp.where(used & ~on_path & ~own_lane, 1.0, 0.0)
    table_k = jnp.where(own_lane, -BIG, 0.0)
    tokens = seg.shape[1]
    member = seg[...] == lax.broadcasted_iota(jnp.int32, (n_segs, tokens), 0)
    member = jnp.where(member, 1.0, 0.0)
    turned = (((0,), (0,)), ((), ()))
    ext = lax.dot_general(member, table_q, turned, preferred_element_type=F32)
    qext[...] = ext.reshape(qext.shape)
    ext = lax.dot_general(member, table_k, turned, preferred_element_type=F32)
    kext[...] = ext.reshape(kext.shape)

    def project(c):
        x = normed[c]
        low = lax.broadcasted_iota(jnp.int32, (rows, 128), 1) < HD
        q = dot(x, w[0]).astype(BF16).astype(F32) * HD ** (-0.5)
        k = dot(x, w[1])
        v = dot(x, w[2])
        q_more, k_more = qext[c], kext[c]
        for i in range(heads // 2):
            part = slice(i * 128, (i + 1) * 128)
            qa[2 * i, c] = jnp.where(low, q[:, part], q_more).astype(BF16)
            qa[2 * i + 1, c] = jnp.where(low, q_more, q[:, part]).astype(BF16)
            ka[2 * i, c] = jnp.where(low, k[:, part], k_more).astype(BF16)
            ka[2 * i + 1, c] = jnp.where(low, k_more, k[:, part]).astype(BF16)
            va[2 * i, c] = jnp.where(low, v[:, part], 1.0).astype(BF16)
            va[2 * i + 1, c] = jnp.where(low, 1.0, v[:, part]).astype(BF16)

    def widen_page(g, source, i):
        lane = lax.broadcasted_iota(jnp.int32, (page_len, 128), 1)
        low, slot = lane < HD, lax.broadcasted_iota(jnp.int32, (page_len, 128), 0)
        lane = lane & (HD - 1)
        hidden = (lane == page_node[g]) | ((lane == n_nodes) & (slot >= page_fill[g]))
        more = jnp.where(hidden, -BIG, 0.0)
        at = pl.ds(pl.multiple_of(g * page_len, page_len), page_len)
        for j in range(heads // 2):
            part = slice(j * 128, (j + 1) * 128)
            k = cache_all[source, 0, i, :, part].astype(F32)
            v = cache_all[source, 1, i, :, part].astype(F32)
            kp[2 * j, :, at] = jnp.where(low, k, more).T.astype(BF16)
            kp[2 * j + 1, :, at] = jnp.where(low, more, k).T.astype(BF16)
            vp[2 * j, g] = jnp.where(low, v, 1.0).astype(BF16)
            vp[2 * j + 1, g] = jnp.where(low, 1.0, v).astype(BF16)

    def take_cache():
        cache_all[p] = cache[...]

        @pl.loop(0, half)
        def _(k):
            first = 2 * chip(k)
            source, other = first + core, first + 1 - core

            @pl.when(k > 0)
            def _():
                c_copy(cache, source, c_send.at[k], sibling).wait_recv()
                c_copy(cache_all.at[source], source, c_fwd.at[k], sibling).start()

            c_copy(cache, other, c_fwd.at[0], sibling).wait_recv()
            for n in range(2):
                for i in range(dev_pages):
                    widen_page((first + n) * dev_pages + i, first + n, i)

    n_keys = n_page * dev_pages * page_len
    block = min(KEY_BLOCK, n_keys)
    block_pages = block // page_len
    blocks = n_keys // block

    def prefix_head(c, i):
        s = dot(qa[i, c], kp[i, :, :block])
        m = jnp.max(s, axis=1, keepdims=True)
        acc[i, c] = dot(weigh(s, m), vp[i, :block_pages].reshape(block, 128))
        top[i, c] = jnp.broadcast_to(m, (rows, 128))
        if blocks > 1:

            @pl.loop(1, blocks)
            def _(b):
                s = dot(qa[i, c], kp[i, :, pl.ds(pl.multiple_of(b * block, block), block)])
                old = top[i, c][:, :1]
                m = jnp.maximum(old, jnp.max(s, axis=1, keepdims=True))
                v = vp[i, pl.ds(b * block_pages, block_pages)].reshape(block, 128)
                acc[i, c] = acc[i, c] * jnp.exp(old - m) + dot(weigh(s, m), v)
                top[i, c] = jnp.broadcast_to(m, (rows, 128))

    def prefix(c):
        @pl.loop(0, heads // 2)
        def _(pair):
            for i in (2 * pair, 2 * pair + 1):
                prefix_head(c, i)

    def finish(c):
        before = jnp.maximum(c - 1, 0)
        shut = jnp.where(c > 0, 0.0, -BIG)
        low = lax.broadcasted_iota(jnp.int32, (rows, 128), 1) < HD
        at = lax.broadcasted_iota(jnp.int32, (rows, rows), 0)
        seen = lax.broadcasted_iota(jnp.int32, (rows, rows), 1) <= at

        def one(i):
            q = qa[i, c]
            near = jnp.where(seen, dot_t(q, ka[i, c]), -BIG)
            far = dot_t(q, ka[i, before]) + shut
            old = top[i, c][:, :1]
            m = jnp.maximum(old, jnp.max(jnp.maximum(near, far), axis=1, keepdims=True))
            total = (
                acc[i, c] * jnp.exp(old - m)
                + dot(weigh(near, m), va[i, c])
                + dot(weigh(far, m), va[i, before])
            )
            return total / pltpu.roll(total, HD, 1)

        for i in range(heads // 2):
            pair = jnp.where(low, one(2 * i), one(2 * i + 1))
            attn[c, :, i * 128 : (i + 1) * 128] = pair.astype(BF16)

        @pl.when(c != h)
        def _():
            a_copy(c, lax.rem(h - c + n_head, n_head)).start()

    def share_w():
        for d in range(1, n_head):
            wz_copy(d).wait_recv()

        @pl.loop(1, SPLIT)
        def _(k):
            wp_copy(my_slice, lax.rem(my_slice + k, SPLIT)).start()

    w_copy.wait()

    @pl.loop(0, n_head)
    def _(r):
        left, right = h - r, h + r
        has_left = left >= 0
        has_right = (right < n_head) & (r > 0)

        @pl.when(has_left & (r > 0))
        def _():
            x_copy(left, 1, h).wait_recv()

            @pl.when(h < n_head - 1)
            def _():
                x_copy(left, 1, h + 1).start()

        @pl.when(has_right)
        def _():
            x_copy(right, 0, h).wait_recv()

            @pl.when(h > 0)
            def _():
                x_copy(right, 0, h - 1).start()

        @pl.loop(0, 2)
        def _(j):
            @pl.when((has_left & (j == 0)) | (has_right & (j == 1)))
            def _():
                project(h + (2 * j - 1) * r)

        @pl.when(r == 0)
        def _():
            take_cache()

        @pl.when(r == 1)
        def _():
            share_w()

        @pl.loop(0, 4)
        def _(j):
            side = 2 * (j & 1) - 1
            far = jnp.where(r == 1, 0, jnp.where(j < 2, r - 1, r))
            c = h + side * far
            ok = ((r == 1) & (j == 0)) | ((r == 2) & (c >= 0) & (c < n_head))
            ok = ok | ((r > 2) & (j >= 2) & (c >= 0) & (c < n_head))

            @pl.when(ok)
            def _():
                prefix(c)

            ripe = ok & ((j != 2) | (c == 0))
            ripe = ripe | ((r > 2) & (j == 0) & (c > 0))

            @pl.when(ripe)
            def _():
                finish(c)

    total = dot(attn[h], wo[...])

    @pl.loop(1, SPLIT)
    def _(k):
        owner = lax.rem(my_slice + k, SPLIT)
        wp_copy(owner, my_slice).wait_recv()

    for d in range(1, n_head):
        a_copy(h, d).wait_recv()
        total = total + dot(attn_rel[d - 1], wo_rel[d - 1])
    out[...] = total.astype(BF16)

    @pl.loop(0, n_head)
    def _(c):
        @pl.when((h > 0) & (c >= h))
        def _():
            x_copy(c, 0, h).wait_send()

        @pl.when((h < n_head - 1) & (c <= h))
        def _():
            x_copy(c, 1, h).wait_send()

        @pl.when(c != h)
        def _():
            a_copy(c, 1).wait_send()

    @pl.loop(1, half)
    def _(k):
        c_copy(cache, p, c_send.at[k], sibling).wait_send()

    @pl.loop(0, half)
    def _(k):
        c_copy(cache, p, c_fwd.at[k], sibling).wait_send()

    for d in range(1, n_head):
        wz_copy(d).wait_send()

    @pl.loop(1, SPLIT)
    def _(k):
        wp_copy(my_slice, lax.rem(my_slice + k, SPLIT)).wait_send()


def shards(
    n_head,
    n_page,
    hidden_in,
    norm_gain,
    w_qkv,
    w_out,
    cache_kv,
    page_node,
    page_fill,
    node_parent,
    tok_seg,
    req_leaf,
):
    rows, model = hidden_in.shape[1:]
    width = w_qkv.shape[2]
    heads = width // HD
    dev_pages, page_len = cache_kv.shape[1:3]
    pages = n_page * dev_pages
    vmem = pl.BlockSpec(memory_space=pltpu.VMEM)
    smem = pl.BlockSpec(memory_space=pltpu.SMEM)
    dma = pltpu.SemaphoreType.DMA
    dims = (n_head, n_page, node_parent.shape[0], req_leaf.shape[1])
    flops = 2 * n_head * rows * (4 * model * width + 4 * heads * 64 * pages * page_len)
    result = pl.pallas_call(
        functools.partial(kernel, dims),
        out_shape=jax.ShapeDtypeStruct((rows, model), BF16),
        in_specs=[vmem] * 2 + [pl.BlockSpec(memory_space=pl.ANY)] + [vmem] * 2 + [smem] * 3 + [vmem, smem],
        out_specs=vmem,
        scratch_shapes=[
            pltpu.VMEM((n_head, rows, model), BF16),
            pltpu.VMEM((n_page,) + cache_kv.shape, BF16),
            pltpu.VMEM((n_head - 1, width, model), BF16),
            pltpu.VMEM((heads, n_head, rows, 128), BF16),
            pltpu.VMEM((heads, n_head, rows, 128), BF16),
            pltpu.VMEM((heads, n_head, rows, 128), BF16),
            pltpu.VMEM((heads, 128, pages * page_len), BF16),
            pltpu.VMEM((heads, pages, page_len, 128), BF16),
            pltpu.VMEM((heads, n_head, rows, 128), F32),
            pltpu.VMEM((heads, n_head, rows, 128), F32),
            pltpu.VMEM((n_head, rows, 128), F32),
            pltpu.VMEM((n_head, rows, 128), F32),
            pltpu.VMEM((n_head, rows, width), BF16),
            pltpu.VMEM((n_head - 1, rows, width), BF16),
            pltpu.VMEM((3, model, width), BF16),
            dma,
            dma((2, n_head)),
            dma((n_head,)),
            dma((n_page // 2,)),
            dma((n_page // 2,)),
            dma((n_page,)),
            dma((n_head - 1,)),
            dma((n_head - 1,)),
            dma((SPLIT,)),
            dma((SPLIT,)),
            dma((n_head,)),
            dma((n_head - 1,)),
        ],
        compiler_params=pltpu.CompilerParams(
            collective_id=0, has_side_effects=True, vmem_limit_bytes=60 * 1024 * 1024
        ),
        cost_estimate=pl.CostEstimate(
            flops=flops, bytes_accessed=4 * 1024 * 1024, transcendentals=0
        ),
    )(
        hidden_in[0],
        norm_gain.reshape(1, model),
        jnp.transpose(w_qkv, (1, 0, 2)),
        w_out,
        cache_kv,
        page_node,
        page_fill,
        node_parent,
        tok_seg,
        req_leaf,
    )
    return result[None]


def solution(mesh):
    placed = (
        P("page", "head", None),
        P(),
        P(None, None, "head"),
        P("head", None),
        P(None, "page", None, "head"),
        P(),
        P(),
        P(),
        P("page", None),
        P("page", None),
    )
    body = functools.partial(shards, mesh.shape["head"], mesh.shape["page"])
    return jax.shard_map(
        body, mesh=mesh, in_specs=placed, out_specs=P("page", "head", None), check_vma=False
    )
```
